512 devices in a mesh: dp: 32 (over y, z_hi, x), tensor: 16 (over z_lo, core).
Axes of the slice: x: 4, y: 4, z: 16 (z_hi: 2, z_lo: 8; z = z_hi * 8 + z_lo), core: 2. Of those that a mesh axis runs over, the one named last changes fastest.
Arguments:
- activations: bfloat16 [4096, 4096], P('dp'), may hold values from -6 to 6
- act_basis: bfloat16 [4096, 4096], P('tensor'), may hold values from -0.09375 to 0.09375
- out_grads: bfloat16 [4096, 14336], P('dp', 'tensor'), may hold values from -3 to 3
- grad_basis: bfloat16 [14336, 14336], P('dp', 'tensor'), may hold values from -0.046875 to 0.046875
Outputs:
- rotated_gradient: float32 [14336, 4096], P('dp', 'tensor')
- scaling: float32 [14336, 4096], P('dp', 'tensor')
The draws below stay inside these ranges and needn't reach their ends.
All inputs are finite; a program needn't handle non-finite values.
Results may differ from the reference program's by a relative error of at most 0.035.
Values may be sent and summed in bfloat16 or wider, within the bound.
No kernel may reach another device: no remote copies, remote signals or barrier semaphores. Data moves between devices by JAX's collectives and lax.ppermute only.
A program may use at most 64 MiB of HBM per device.

```python
import jax
import jax.numpy as jnp
from jax import lax

D = 4096
FF = 14336
TOKENS = 4096
N_TENSOR = 16


def block_levels(rng, dims, split, least, top_value):
    level, own = 1.0, jax.random.fold_in(rng, 6)
    for dim, blocks in split:
        steps = jnp.exp(jax.random.uniform(jax.random.fold_in(own, dim), (blocks,), jnp.float32, least / len(split), top_value / len(split)))
        level = level * jnp.repeat(steps, dims[dim] // blocks).reshape([-1 if axis == dim else 1 for axis in range(len(dims))])
    return level


def centred(own_key, shape, deviation, reach, split=(), held_as=jnp.bfloat16):
    level = block_levels(own_key, shape, split, -0.22, 0.18) if split else 1.0
    entries = jax.random.normal(own_key, shape, jnp.float32) * deviation * level
    return jnp.minimum(jnp.maximum(entries, -reach), reach).astype(held_as)


def setup_inputs(seed: int = 0) -> dict:
    seeds = jax.random.split(jax.random.key(seed), 5)
    activations = centred(seeds[0], (TOKENS, D), 1.0, 6.0, ((0, 32),))
    act_basis = centred(seeds[1], (D, D), D ** -0.5, 0.09375, ((0, 16),))
    out_grads = centred(seeds[2], (TOKENS, FF), 0.5, 3.0, ((0, 32), (1, 16)))
    grad_basis = centred(seeds[3], (FF, FF), FF ** -0.5, 0.046875, ((0, 32), (1, 16)))
    return dict(activations=activations, act_basis=act_basis, out_grads=out_grads, grad_basis=grad_basis)


def square_round(values):
    wide = values.astype(jnp.float32)
    return (wide * wide).astype(jnp.bfloat16)


def reference(activations, act_basis, out_grads, grad_basis):
    rotated_acts = jnp.dot(activations.astype(jnp.float32), act_basis.astype(jnp.float32).T).astype(jnp.bfloat16)
    act_squares = square_round(rotated_acts)
    width = FF // N_TENSOR

    def add_block(total, index):
        start = (index * width).astype(jnp.int32)
        basis_cols = lax.dynamic_slice_in_dim(grad_basis, start, width, 1).astype(jnp.float32)
        grad_cols = lax.dynamic_slice_in_dim(out_grads, start, width, 1).astype(jnp.float32)
        block_sum = jnp.dot(basis_cols, grad_cols.T).astype(jnp.bfloat16)
        block_sum = lax.optimization_barrier(block_sum)
        return total + block_sum.astype(jnp.float32), None

    total, _ = lax.scan(add_block, jnp.zeros((FF, TOKENS), jnp.float32), jnp.arange(N_TENSOR, dtype=jnp.int32))
    rotated_grads = total.astype(jnp.bfloat16)
    grad_squares = square_round(rotated_grads)
    rotated_gradient = jnp.dot(rotated_grads.astype(jnp.float32), rotated_acts.astype(jnp.float32))
    scaling = jnp.dot(grad_squares.astype(jnp.float32), act_squares.astype(jnp.float32)) / TOKENS
    return rotated_gradient, scaling
```

```python
import jax
import jax.numpy as jnp
from jax import lax
from jax.experimental import pallas as pl
from jax.experimental.pallas import tpu as pltpu
from jax.sharding import Mesh, PartitionSpec as P

F32 = jnp.float32
BF16 = jnp.bfloat16
NX, NY, NM = 4, 4, 4
VMEM = pl.BlockSpec(memory_space=pltpu.VMEM)
SMEM = pl.BlockSpec(memory_space=pltpu.SMEM)


def params():
    return pltpu.CompilerParams(vmem_limit_bytes=40 * 1024 * 1024)


def cost(flops, nbytes):
    return pl.CostEstimate(flops=flops, bytes_accessed=nbytes, transcendentals=0)


def from_rel(value, axis, step, size):
    return lax.ppermute(value, axis, [((i + step) % size, i) for i in range(size)])


def block_kernel(where_ref, *refs):
    tokens, basis = refs[:8], refs[8:12]
    own_ref, other_ref, half_ref = refs[12:]
    here, half, parity = where_ref[0], where_ref[1], where_ref[2]
    rows = tokens[0].shape[0]
    for j in range(NY):

        @pl.when(half == 0)
        def _():
            half_ref[j * rows : (j + 1) * rows] = tokens[j][...]

        @pl.when(half == 1)
        def _():
            half_ref[j * rows : (j + 1) * rows] = tokens[NY + j][...]

    width = 2 * rows
    for j in range(NX):
        home = lax.rem(here + j, NX)
        left = basis[j][...]
        for rel, out in ((1, other_ref), (0, own_ref)):
            start = pl.multiple_of(lax.rem(parity + rel, 2) * width, width)
            right = half_ref[pl.ds(start, width)]
            out[home] = lax.dot_general(
                left, right, (((1,), (1,)), ((), ())), preferred_element_type=F32
            ).astype(BF16)


def block_sums(where, tokens, basis):
    rows, depth = tokens[0].shape
    crows = basis[0].shape[0]
    shape = jax.ShapeDtypeStruct((NX, crows, 2 * rows), BF16)
    return pl.pallas_call(
        block_kernel,
        out_shape=(shape, shape),
        in_specs=[SMEM] + [VMEM] * 12,
        out_specs=(VMEM, VMEM),
        scratch_shapes=[pltpu.VMEM((NY * rows, depth), BF16)],
        compiler_params=params(),
        cost_estimate=cost(2 * NX * crows * NY * rows * depth, 9 * 2**20),
        name="block_sums",
    )(where, *tokens, *basis)


def final_kernel(where_ref, mine_ref, mate_ref, acts_ref, grad_ref, scale_ref):
    y, core = where_ref[0], where_ref[1]
    pairs, _, _, piece, width = mine_ref.shape
    rows = acts_ref.shape[3]
    total_tokens = 2 * NY * NX * rows
    first = True
    for side, ref in ((0, mine_ref), (1, mate_ref)):
        half = lax.rem(core + side, 2)
        for parity in range(2):
            for x in range(NX):
                g = ref[:, parity, x].reshape(pairs * piece, width)
                a = jnp.concatenate(
                    [acts_ref[lax.rem(y + 2 * parity + n, NY), x, half] for n in range(2)], axis=0
                )
                gw, aw = g.astype(F32), a.astype(F32)
                g2, a2 = (gw * gw).astype(BF16), (aw * aw).astype(BF16)
                p1 = jnp.dot(g, a, preferred_element_type=F32)
                p2 = jnp.dot(g2, a2, preferred_element_type=F32)
                if first:
                    grad_ref[...] = p1
                    scale_ref[...] = p2
                    first = False
                else:
                    grad_ref[...] += p1
                    scale_ref[...] += p2
    scale_ref[...] = scale_ref[...] / total_tokens


def final(where, mine, mate, acts):
    pairs, _, _, piece, width = mine.shape
    shape = jax.ShapeDtypeStruct((pairs * piece, acts.shape[-1]), F32)
    return pl.pallas_call(
        final_kernel,
        out_shape=(shape, shape),
        in_specs=[SMEM, VMEM, VMEM, VMEM],
        out_specs=(VMEM, VMEM),
        compiler_params=params(),
        cost_estimate=cost(4 * 448 * 4096 * 256, 7 * 2**20),
        name="final_products",
    )(where, mine, mate, acts)


def added(*values):
    total = values[0].astype(F32)
    for v in values[1:]:
        total = total + v.astype(F32)
    return total.astype(BF16)


def body(activations, act_basis, out_grads, grad_basis):
    x, y, core, parity = (lax.axis_index(a) for a in ("x", "y", "c", "p"))
    other_half = lax.ppermute(out_grads, "h", [(0, 1), (1, 0)])
    tokens = [out_grads] + [from_rel(out_grads, "y", j, NY) for j in (1, 2, 3)]
    basis = [grad_basis] + [from_rel(grad_basis, "x", j, NX) for j in (1, 2, 3)]
    tokens += [other_half] + [from_rel(other_half, "y", j, NY) for j in (1, 2, 3)]

    acts = lax.dot_general(
        activations, act_basis, (((1,), (1,)), ((), ())), preferred_element_type=F32
    ).astype(BF16)
    both = jnp.stack([acts, lax.ppermute(acts, "h", [(0, 1), (1, 0)])])
    all_acts = lax.all_gather(both, ("y", "x"), axis=0, tiled=False)
    all_acts = all_acts.reshape(NY, NX, *both.shape)

    swap = lambda v, axis: lax.ppermute(v, axis, [(0, 1), (1, 0)])
    send_own, send_other = block_sums(jnp.stack([x, 1 - core, parity]).astype(jnp.int32), tokens, basis)
    got_other = swap(send_other, "c")
    got_own = swap(send_own, "c")
    mine_own, mine_other = block_sums(jnp.stack([x, core, parity]).astype(jnp.int32), tokens, basis)
    pair = swap(added(mine_other, got_other), "p")
    partial = added(mine_own, got_own, pair)
    crows, width = partial.shape[1:]
    piece = crows // NM
    spread = lax.all_to_all(
        partial.reshape(NX * NM, piece, width), ("x", "m"), split_axis=0, concat_axis=0, tiled=True
    ).reshape(NX, NM, piece, width)
    own = added(*[spread[:, j] for j in range(NM)])
    mine = lax.all_gather(own, ("m", "p"), axis=0, tiled=False).reshape(NM, 2, NX, piece, width)
    mate = swap(mine, "c")
    return final(jnp.stack([y, core]).astype(jnp.int32), mine, mate, all_acts)


def solution(mesh):
    fine = Mesh(mesh.devices.reshape(NY, 2, NX, NM, 2, 2), ("y", "h", "x", "m", "p", "c"))
    dp, tensor = ("y", "h", "x"), ("m", "p", "c")
    return jax.shard_map(
        body,
        mesh=fine,
        in_specs=(P(dp, None), P(tensor, None), P(dp, tensor), P(dp, tensor)),
        out_specs=(P(dp, tensor), P(dp, tensor)),
        check_vma=False,
    )
```

```python
import jax
import jax.numpy as jnp
from jax import lax
from jax.experimental import pallas as pl
from jax.experimental.pallas import tpu as pltpu
from jax.sharding import Mesh, PartitionSpec as P

F32 = jnp.float32
BF16 = jnp.bfloat16
NX, NY, NM = 4, 4, 4
VMEM = pl.BlockSpec(memory_space=pltpu.VMEM)
SMEM = pl.BlockSpec(memory_space=pltpu.SMEM)


def params():
    return pltpu.CompilerParams(vmem_limit_bytes=24 * 1024 * 1024)


def cost(flops, nbytes):
    return pl.CostEstimate(flops=flops, bytes_accessed=nbytes, transcendentals=0)


def from_rel(value, axis, step, size):
    return lax.ppermute(value, axis, [((i + step) % size, i) for i in range(size)])


def block_kernel(where_ref, *refs):
    tokens, basis_ref, out_ref = refs[:NY], refs[NY], refs[NY + 1]
    half = where_ref[1]
    rows = tokens[0].shape[1]
    piece = basis_ref.shape[1] // NM
    for j in range(NX):
        for parity in range(2):
            right = jnp.concatenate([tokens[2 * parity + n][half] for n in range(2)], axis=0)
            sums = lax.dot_general(
                basis_ref[j], right, (((1,), (1,)), ((), ())), preferred_element_type=F32
            ).astype(BF16)
            for m in range(NM):
                out_ref[2 * m + parity, j] = sums[m * piece : (m + 1) * piece]


def block_sums(where, tokens, basis):
    _, rows, depth = tokens[0].shape
    crows = basis.shape[1]
    return pl.pallas_call(
        block_kernel,
        out_shape=jax.ShapeDtypeStruct((2 * NM, NX, crows // NM, 2 * rows), BF16),
        in_specs=[SMEM] + [VMEM] * (NY + 1),
        out_specs=VMEM,
        compiler_params=params(),
        cost_estimate=cost(2 * NX * crows * NY * rows * depth, 9 * 2**20),
        name="block_sums",
    )(where, *tokens, basis)


def final_kernel(where_ref, mine_ref, mate_ref, *refs):
    acts, (grad_ref, scale_ref) = refs[:NX], refs[NX:]
    here, core = where_ref[0], where_ref[1]
    pairs, _, _, piece, width = mine_ref.shape
    rows = acts[0].shape[2]
    first = True
    for side, ref in ((0, mine_ref), (1, mate_ref)):
        half = lax.rem(core + side, 2)
        for j in range(NX):
            home = lax.rem(here + j, NX)
            for parity in range(2):
                g = ref[:, parity, home].reshape(pairs * piece, width)
                a = acts[j][2 * parity : 2 * parity + 2, half].reshape(2 * rows, -1)
                gw, aw = g.astype(F32), a.astype(F32)
                g2, a2 = (gw * gw).astype(BF16), (aw * aw).astype(BF16)
                p1 = jnp.dot(g, a, preferred_element_type=F32)
                p2 = jnp.dot(g2, a2, preferred_element_type=F32)
                if first:
                    grad_ref[...] = p1
                    scale_ref[...] = p2
                    first = False
                else:
                    grad_ref[...] += p1
                    scale_ref[...] += p2
    scale_ref[...] = scale_ref[...] / (2 * NY * NX * rows)


def final(where, mine, mate, acts):
    pairs, _, _, piece, width = mine.shape
    shape = jax.ShapeDtypeStruct((pairs * piece, acts[0].shape[-1]), F32)
    return pl.pallas_call(
        final_kernel,
        out_shape=(shape, shape),
        in_specs=[SMEM] + [VMEM] * (2 + NX),
        out_specs=(VMEM, VMEM),
        compiler_params=params(),
        cost_estimate=cost(4 * 448 * 4096 * 256, 7 * 2**20),
        name="final_products",
    )(where, mine, mate, *acts)


def added(*values):
    total = values[0].astype(F32)
    for v in values[1:]:
        total = total + v.astype(F32)
    return total.astype(BF16)


def body(activations, act_basis, out_grads, grad_basis):
    x, core = lax.axis_index("x"), lax.axis_index("c")
    swap = lambda v, axis: lax.ppermute(v, axis, [(0, 1), (1, 0)])
    basis = lax.all_gather(grad_basis, "x", axis=0, tiled=False)
    halves = jnp.stack([out_grads, swap(out_grads, "h")])
    tokens = [halves] + [from_rel(halves, "y", j, NY) for j in (1, 2, 3)]

    send = block_sums(jnp.stack([x, 1 - core]).astype(jnp.int32), tokens, basis)
    got = swap(send, "c")
    mine = block_sums(jnp.stack([x, core]).astype(jnp.int32), tokens, basis)
    partial = added(mine, got)

    activations, partial = lax.optimization_barrier((activations, partial))
    acts = lax.dot_general(
        activations, act_basis, (((1,), (1,)), ((), ())), preferred_element_type=F32
    ).astype(BF16)
    both = jnp.stack([acts, swap(acts, "h")])
    column = jnp.stack([both] + [from_rel(both, "y", j, NY) for j in (1, 2, 3)])
    all_acts = [column] + [from_rel(column, "x", j, NX) for j in (1, 2, 3)]

    own = lax.psum_scatter(partial, ("m", "p"), scatter_dimension=0, tiled=False)
    own, all_acts = lax.optimization_barrier((own, all_acts))
    own = lax.all_to_all(own, "x", split_axis=0, concat_axis=0, tiled=True)
    mine = lax.all_gather(own, ("m", "p"), axis=0, tiled=False).reshape(NM, 2, *own.shape)
    mate = swap(mine, "c")
    return final(jnp.stack([x, core]).astype(jnp.int32), mine, mate, all_acts)


def solution(mesh):
    fine = Mesh(mesh.devices.reshape(NY, 2, NX, NM, 2, 2), ("y", "h", "x", "m", "p", "c"))
    dp, tensor = ("y", "h", "x"), ("m", "p", "c")
    return jax.shard_map(
        body,
        mesh=fine,
        in_specs=(P(dp, None), P(tensor, None), P(dp, tensor), P(dp, tensor)),
        out_specs=(P(dp, tensor), P(dp, tensor)),
        check_vma=False,
    )
```

```python
import functools

import jax
import jax.numpy as jnp
from jax import lax
from jax.experimental import pallas as pl
from jax.experimental.pallas import tpu as pltpu
from jax.sharding import Mesh, PartitionSpec as P

F32 = jnp.float32
BF16 = jnp.bfloat16
NX, NY, NM = 4, 4, 4
VMEM = pl.BlockSpec(memory_space=pltpu.VMEM)
SMEM = pl.BlockSpec(memory_space=pltpu.SMEM)


def params():
    return pltpu.CompilerParams(vmem_limit_bytes=24 * 1024 * 1024)


def cost(flops, nbytes):
    return pl.CostEstimate(flops=flops, bytes_accessed=nbytes, transcendentals=0)


def from_rel(value, axis, step, size):
    return lax.ppermute(value, axis, [((i + step) % size, i) for i in range(size)])


def block_kernel(where_ref, *refs):
    tokens, basis_ref, out_ref = refs[:NY], refs[NY], refs[NY + 1]
    half = where_ref[1]
    rows = tokens[0].shape[1]
    piece = basis_ref.shape[1] // NM
    for j in range(NX):
        for parity in range(2):
            right = jnp.concatenate([tokens[2 * parity + n][half] for n in range(2)], axis=0)
            sums = lax.dot_general(
                basis_ref[j], right, (((1,), (1,)), ((), ())), preferred_element_type=F32
            ).astype(BF16)
            for m in range(NM):
                out_ref[2 * m + parity, j] = sums[m * piece : (m + 1) * piece]


def block_sums(where, tokens, basis):
    _, rows, depth = tokens[0].shape
    crows = basis.shape[1]
    return pl.pallas_call(
        block_kernel,
        out_shape=jax.ShapeDtypeStruct((2 * NM, NX, crows // NM, 2 * rows), BF16),
        in_specs=[SMEM] + [VMEM] * (NY + 1),
        out_specs=VMEM,
        compiler_params=params(),
        cost_estimate=cost(2 * NX * crows * NY * rows * depth, 9 * 2**20),
        name="block_sums",
    )(where, *tokens, basis)


def add_products(out1, out2, first, pieces, acts, cols):
    for j in range(NX):
        g, a = pieces(j), acts(j)[:, cols]
        gw, aw = g.astype(F32), a.astype(F32)
        g2, a2 = (gw * gw).astype(BF16), (aw * aw).astype(BF16)
        p1 = jnp.dot(g, a, preferred_element_type=F32)
        p2 = jnp.dot(g2, a2, preferred_element_type=F32)
        if first and j == 0:
            out1[...] = p1
            out2[...] = p2
        else:
            out1[...] += p1
            out2[...] += p2


def pieces_of(ref):
    pairs, _, piece, width = ref.shape
    return lambda j: ref[:, j].reshape(pairs * piece, width)


def acts_of(refs, here, half):
    rows, cols = refs[0].shape[2:]

    def at(j):
        return refs[j][:, half].reshape(2 * rows, cols)

    return at


def near_kernel(where_ref, mine_ref, *refs):
    acts, (p1_ref, p2_ref) = refs[:NX], refs[NX:]
    here, core = where_ref[0], where_ref[1]
    side = pieces_of(mine_ref)
    add_products(
        p1_ref, p2_ref, True, lambda j: side(lax.rem(here + j, NX)), acts_of(acts, here, core), slice(None)
    )


def far_kernel(keep, where_ref, mate_ref, p1_ref, p2_ref, *refs):
    acts, outs = refs[:NX], refs[NX:]
    acc1, acc2 = outs[-2:]
    here, core = where_ref[0], where_ref[1]
    half = acc1.shape[1]
    cols = slice(0, half) if keep else slice(half, 2 * half)
    acc1[...] = p1_ref[:, cols]
    acc2[...] = p2_ref[:, cols]
    side = pieces_of(mate_ref)
    add_products(
        acc1, acc2, False, lambda j: side(lax.rem(here + j, NX)), acts_of(acts, here, 1 - core), cols
    )
    total = 2 * NY * NX * acts[0].shape[2]
    if keep:
        acc2[...] = acc2[...] / total
    else:
        outs[0][0] = acc1[...].astype(BF16)
        outs[0][1] = (acc2[...] / total).astype(BF16)


def near_products(where, mine, acts):
    pairs, _, piece, width = mine.shape
    shape = jax.ShapeDtypeStruct((pairs * piece, acts[0].shape[-1]), F32)
    return pl.pallas_call(
        near_kernel,
        out_shape=(shape, shape),
        in_specs=[SMEM] + [VMEM] * (1 + NX),
        out_specs=(VMEM, VMEM),
        compiler_params=params(),
        cost_estimate=cost(4 * 448 * 1024 * 512, 5 * 2**20),
        name="near_products",
    )(where, mine, *acts)


def far_products(keep, where, mate, p1, p2, acts):
    crows, cols = p1.shape
    shape = jax.ShapeDtypeStruct((crows, cols // 2), F32)
    return pl.pallas_call(
        functools.partial(far_kernel, keep),
        out_shape=(shape, shape) if keep else jax.ShapeDtypeStruct((2, crows, cols // 2), BF16),
        in_specs=[SMEM] + [VMEM] * (3 + NX),
        out_specs=(VMEM, VMEM) if keep else VMEM,
        scratch_shapes=[] if keep else [pltpu.VMEM((crows, cols // 2), F32)] * 2,
        compiler_params=params(),
        cost_estimate=cost(2 * 448 * 1024 * 512, 5 * 2**20),
        name="far_products",
    )(where, mate, p1, p2, *acts)


def added(*values):
    total = values[0].astype(F32)
    for v in values[1:]:
        total = total + v.astype(F32)
    return total.astype(BF16)


def own_columns(value, parity):
    rows = [((i + 2) % NY * 2 + 1, i * 2 + 1) for i in range(NY)]
    first = jnp.where(parity == 0, value, lax.ppermute(value, ("y", "p"), rows))
    rows = [((i + 1 + 2 * p) % NY * 2 + p, i * 2 + p) for i in range(NY) for p in range(2)]
    return jnp.stack([first, lax.ppermute(value, ("y", "p"), rows)])


def body(activations, act_basis, out_grads, grad_basis):
    x, core, parity = (lax.axis_index(a) for a in ("x", "c", "p"))
    swap = lambda v, axis: lax.ppermute(v, axis, [(0, 1), (1, 0)])
    pack = lambda *v: jnp.stack(v).astype(jnp.int32)
    basis = lax.all_gather(grad_basis, "x", axis=0, tiled=False)
    halves = jnp.stack([out_grads, swap(out_grads, "h")])
    tokens = [halves] + [from_rel(halves, "y", j, NY) for j in (1, 2, 3)]

    acts = lax.dot_general(
        activations, act_basis, (((1,), (1,)), ((), ())), preferred_element_type=F32
    ).astype(BF16)
    acts = jnp.stack([acts, swap(acts, "h")])
    *tokens, acts = lax.optimization_barrier((*tokens, acts))

    send = block_sums(pack(x, 1 - core), tokens, basis)
    got = swap(send, "c")
    mine = block_sums(pack(x, core), tokens, basis)
    partial = added(mine, got)

    acts, partial = lax.optimization_barrier((acts, partial))
    acts = own_columns(jnp.concatenate([acts, swap(acts, "p")], axis=-1), parity)
    all_acts = [acts] + [from_rel(acts, "x", j, NX) for j in (1, 2, 3)]

    own = lax.psum_scatter(partial, ("m", "p"), scatter_dimension=0, tiled=False)
    own, all_acts = lax.optimization_barrier((own, all_acts))
    own = lax.all_to_all(own, "x", split_axis=0, concat_axis=0, tiled=True)
    mine = lax.all_gather(own, "m", axis=0, tiled=False)
    mate = swap(mine, "c")
    where = pack(x, core)
    p1, p2 = near_products(where, mine, all_acts)
    away = swap(far_products(False, where, mate, p1, p2, all_acts), "p")
    grad, scale = far_products(True, where, mate, p1, p2, all_acts)
    return grad + away[0].astype(F32), scale + away[1].astype(F32)


def solution(mesh):
    fine = Mesh(mesh.devices.reshape(NY, 2, NX, NM, 2, 2), ("y", "h", "x", "m", "p", "c"))
    dp, tensor = ("y", "h", "x"), ("m", "p", "c")
    return jax.shard_map(
        body,
        mesh=fine,
        in_specs=(P(dp, None), P(tensor, None), P(dp, tensor), P(dp, tensor)),
        out_specs=(P(dp, tensor), P(dp, tensor)),
        check_vma=False,
    )
```

```python
import functools

import jax
import jax.numpy as jnp
from jax import lax
from jax.experimental import pallas as pl
from jax.experimental.pallas import tpu as pltpu
from jax.sharding import Mesh, PartitionSpec as P

F32 = jnp.float32
BF16 = jnp.bfloat16
NX, NY, NM = 4, 4, 4
VMEM = pl.BlockSpec(memory_space=pltpu.VMEM)
ANY = pl.BlockSpec(memory_space=pl.ANY)
SMEM = pl.BlockSpec(memory_space=pltpu.SMEM)


def params():
    return pltpu.CompilerParams(vmem_limit_bytes=24 * 1024 * 1024)


def cost(flops, nbytes):
    return pl.CostEstimate(flops=flops, bytes_accessed=nbytes, transcendentals=0)


def from_rel(value, axis, step, size):
    return lax.ppermute(value, axis, [((i + step) % size, i) for i in range(size)])


def block_kernel(rel, where_ref, *refs):
    tokens, basis = refs[:2], refs[2 : 2 + NX]
    out_ref, held_ref = refs[3 + NX :]
    here, y, half, parity = (where_ref[i] for i in range(4))
    rows = tokens[0].shape[1]
    for side in range(2):

        @pl.when(half == side)
        def _():
            for n in range(2):
                source = lax.rem(y + 2 * (parity + rel) + n, NY)
                held_ref[pl.ds(n * rows, rows)] = tokens[side][source]

    for j in range(NX):
        home = lax.rem(here + j, NX)
        out_ref[home] = lax.dot_general(
            basis[j][...], held_ref[...], (((1,), (1,)), ((), ())), preferred_element_type=F32
        ).astype(BF16)


def block_sums(rel, where, tokens, basis, turn):
    _, rows, depth = tokens[0].shape
    crows = basis[0].shape[0]
    return pl.pallas_call(
        functools.partial(block_kernel, rel),
        out_shape=jax.ShapeDtypeStruct((NX, crows, 2 * rows), BF16),
        in_specs=[SMEM] + [VMEM] * (2 + NX) + [ANY],
        out_specs=VMEM,
        scratch_shapes=[pltpu.VMEM((2 * rows, depth), BF16)],
        compiler_params=params(),
        cost_estimate=cost(2 * NX * crows * 2 * rows * depth, 6 * 2**20),
        name="block_sums",
    )(where, *tokens, *basis, turn)


def add_products(out1, out2, first, pieces, acts, cols):
    for j in range(NX):
        g, a = pieces(j), acts(j)[:, cols]
        gw, aw = g.astype(F32), a.astype(F32)
        g2, a2 = (gw * gw).astype(BF16), (aw * aw).astype(BF16)
        p1 = jnp.dot(g, a, preferred_element_type=F32)
        p2 = jnp.dot(g2, a2, preferred_element_type=F32)
        if first and j == 0:
            out1[...] = p1
            out2[...] = p2
        else:
            out1[...] += p1
            out2[...] += p2


def pieces_of(ref):
    pairs, _, piece, width = ref.shape
    return lambda j: ref[:, j].reshape(pairs * piece, width)


def acts_of(refs, here, half):
    rows, cols = refs[0].shape[2:]

    def at(j):
        return refs[j][:, half].reshape(2 * rows, cols)

    return at


def near_kernel(where_ref, mine_ref, *refs):
    acts, (p1_ref, p2_ref) = refs[:NX], refs[NX:]
    here, core = where_ref[0], where_ref[1]
    side = pieces_of(mine_ref)
    add_products(
        p1_ref, p2_ref, True, lambda j: side(lax.rem(here + j, NX)), acts_of(acts, here, core), slice(None)
    )


def far_kernel(keep, where_ref, mate_ref, p1_ref, p2_ref, *refs):
    acts, outs = refs[:NX], refs[NX:]
    acc1, acc2 = outs[-2:]
    here, core = where_ref[0], where_ref[1]
    half = acc1.shape[1]
    cols = slice(0, half) if keep else slice(half, 2 * half)
    acc1[...] = p1_ref[:, cols]
    acc2[...] = p2_ref[:, cols]
    side = pieces_of(mate_ref)
    add_products(
        acc1, acc2, False, lambda j: side(lax.rem(here + j, NX)), acts_of(acts, here, 1 - core), cols
    )
    total = 2 * NY * NX * acts[0].shape[2]
    if keep:
        acc2[...] = acc2[...] / total
    else:
        outs[0][0] = acc1[...].astype(BF16)
        outs[0][1] = (acc2[...] / total).astype(BF16)


def near_products(where, mine, acts):
    pairs, _, piece, width = mine.shape
    shape = jax.ShapeDtypeStruct((pairs * piece, acts[0].shape[-1]), F32)
    return pl.pallas_call(
        near_kernel,
        out_shape=(shape, shape),
        in_specs=[SMEM] + [VMEM] * (1 + NX),
        out_specs=(VMEM, VMEM),
        compiler_params=params(),
        cost_estimate=cost(4 * 448 * 1024 * 512, 5 * 2**20),
        name="near_products",
    )(where, mine, *acts)


def far_products(keep, where, mate, p1, p2, acts):
    crows, cols = p1.shape
    shape = jax.ShapeDtypeStruct((crows, cols // 2), F32)
    return pl.pallas_call(
        functools.partial(far_kernel, keep),
        out_shape=(shape, shape) if keep else jax.ShapeDtypeStruct((2, crows, cols // 2), BF16),
        in_specs=[SMEM] + [VMEM] * (3 + NX),
        out_specs=(VMEM, VMEM) if keep else VMEM,
        scratch_shapes=[] if keep else [pltpu.VMEM((crows, cols // 2), F32)] * 2,
        compiler_params=params(),
        cost_estimate=cost(2 * 448 * 1024 * 512, 5 * 2**20),
        name="far_products",
    )(where, mate, p1, p2, *acts)


def added(*values):
    total = values[0].astype(F32)
    for v in values[1:]:
        total = total + v.astype(F32)
    return total.astype(BF16)


def own_columns(value, parity):
    rows = [((i + 2) % NY * 2 + 1, i * 2 + 1) for i in range(NY)]
    first = jnp.where(parity == 0, value, lax.ppermute(value, ("y", "p"), rows))
    rows = [((i + 1 + 2 * p) % NY * 2 + p, i * 2 + p) for i in range(NY) for p in range(2)]
    return jnp.stack([first, lax.ppermute(value, ("y", "p"), rows)])


def body(activations, act_basis, out_grads, grad_basis):
    x, y, core, parity = (lax.axis_index(a) for a in ("x", "y", "c", "p"))
    swap = lambda v, axis: lax.ppermute(v, axis, [(0, 1), (1, 0)])
    pack = lambda *v: jnp.stack(v).astype(jnp.int32)
    gather = lambda v, axis: lax.all_gather(v, axis, axis=0, tiled=False)
    acts = lax.dot_general(
        activations, act_basis, (((1,), (1,)), ((), ())), preferred_element_type=F32
    ).astype(BF16)
    depth = out_grads.shape[1]
    payload = jnp.concatenate([out_grads, acts], axis=1)
    crossed = swap(payload, "h")
    turn, grad_basis, out_grads = lax.optimization_barrier(
        (swap(payload[:16, :128], "c"), grad_basis, out_grads)
    )
    basis = [grad_basis] + [from_rel(grad_basis, "x", j, NX) for j in (1, 2, 3)]
    tokens = [gather(out_grads, "y"), gather(crossed[:, :depth], "y")]
    acts = jnp.stack([acts, crossed[:, depth:]])
    acts = jnp.concatenate([acts, swap(acts, "p")], axis=-1)
    *tokens, acts = lax.optimization_barrier((*tokens, acts))

    here, there = pack(x, y, core, parity), pack(x, y, 1 - core, parity)
    got = swap(block_sums(1, there, tokens, basis, turn), "c")
    other = added(block_sums(1, here, tokens, basis, turn), got)
    other, acts, *tokens = lax.optimization_barrier((other, acts, *tokens))
    pair = swap(other, "p")
    got = swap(block_sums(0, there, tokens, basis, turn), "c")
    acts = own_columns(acts, parity)
    partial = added(block_sums(0, here, tokens, basis, turn), got, pair)
    partial, acts = lax.optimization_barrier((partial, acts))
    all_acts = [acts] + [from_rel(acts, "x", j, NX) for j in (1, 2, 3)]
    crows, width = partial.shape[1:]
    spread = lax.all_to_all(
        partial.reshape(NX * NM, crows // NM, width), ("x", "m"), split_axis=0, concat_axis=0, tiled=True
    ).reshape(NX, NM, crows // NM, width)
    own = added(*[spread[:, j] for j in range(NM)])
    own, all_acts = lax.optimization_barrier((own, all_acts))
    mine = gather(own, "m")
    mate = swap(mine, "c")
    where = pack(x, core)
    p1, p2 = near_products(where, mine, all_acts)
    away = swap(far_products(False, where, mate, p1, p2, all_acts), "p")
    grad, scale = far_products(True, where, mate, p1, p2, all_acts)
    return grad + away[0].astype(F32), scale + away[1].astype(F32)


def solution(mesh):
    fine = Mesh(mesh.devices.reshape(NY, 2, NX, NM, 2, 2), ("y", "h", "x", "m", "p", "c"))
    dp, tensor = ("y", "h", "x"), ("m", "p", "c")
    return jax.shard_map(
        body,
        mesh=fine,
        in_specs=(P(dp, None), P(tensor, None), P(dp, tensor), P(dp, tensor)),
        out_specs=(P(dp, tensor), P(dp, tensor)),
        check_vma=False,
    )
```

```python
import functools

import jax
import jax.numpy as jnp
from jax import lax
from jax.experimental import pallas as pl
from jax.experimental.pallas import tpu as pltpu
from jax.sharding import Mesh, PartitionSpec as P

F32 = jnp.float32
BF16 = jnp.bfloat16
NX, NY, NM = 4, 4, 4
VMEM = pl.BlockSpec(memory_space=pltpu.VMEM)
ANY = pl.BlockSpec(memory_space=pl.ANY)
SMEM = pl.BlockSpec(memory_space=pltpu.SMEM)


def params():
    return pltpu.CompilerParams(vmem_limit_bytes=24 * 1024 * 1024)


def cost(flops, nbytes):
    return pl.CostEstimate(flops=flops, bytes_accessed=nbytes, transcendentals=0)


def from_rel(value, axis, step, size):
    return lax.ppermute(value, axis, [((i + step) % size, i) for i in range(size)])


def block_kernel(rel, where_ref, *refs):
    tokens, basis = refs[:2], refs[2 : 2 + NX]
    out_ref, held_ref = refs[3 + NX :]
    here, y, half, parity = (where_ref[i] for i in range(4))
    rows = tokens[0].shape[1]
    for side in range(2):

        @pl.when(half == side)
        def _():
            for n in range(2):
                source = lax.rem(y + lax.rem(parity + rel, 2) + 2 * n, NY)
                held_ref[pl.ds(n * rows, rows)] = tokens[side][source]

    for j in range(NX):
        home = lax.rem(here + j, NX)
        out_ref[home] = lax.dot_general(
            basis[j][...], held_ref[...], (((1,), (1,)), ((), ())), preferred_element_type=F32
        ).astype(BF16)


def block_sums(rel, where, tokens, basis, turn):
    _, rows, depth = tokens[0].shape
    crows = basis[0].shape[0]
    return pl.pallas_call(
        functools.partial(block_kernel, rel),
        out_shape=jax.ShapeDtypeStruct((NX, crows, 2 * rows), BF16),
        in_specs=[SMEM] + [VMEM] * (2 + NX) + [ANY],
        out_specs=VMEM,
        scratch_shapes=[pltpu.VMEM((2 * rows, depth), BF16)],
        compiler_params=params(),
        cost_estimate=cost(2 * NX * crows * 2 * rows * depth, 6 * 2**20),
        name="block_sums",
    )(where, *tokens, *basis, turn)


def add_products(out1, out2, first, pieces, acts, cols):
    for j in range(NX):
        g, a = pieces(j), acts(j)[:, cols]
        gw, aw = g.astype(F32), a.astype(F32)
        g2, a2 = (gw * gw).astype(BF16), (aw * aw).astype(BF16)
        p1 = jnp.dot(g, a, preferred_element_type=F32)
        p2 = jnp.dot(g2, a2, preferred_element_type=F32)
        if first and j == 0:
            out1[...] = p1
            out2[...] = p2
        else:
            out1[...] += p1
            out2[...] += p2


def pieces_of(ref):
    pairs, _, piece, width = ref.shape
    return lambda j: ref[:, j].reshape(pairs * piece, width)


def acts_of(refs, half):
    return lambda j: jnp.concatenate([r[j, half] for r in refs], axis=0)


def near_kernel(where_ref, mine_ref, *refs):
    acts, (p1_ref, p2_ref) = refs[:2], refs[2:]
    here, core = where_ref[0], where_ref[1]
    side = pieces_of(mine_ref)
    add_products(
        p1_ref, p2_ref, True, lambda j: side(lax.rem(here + j, NX)), acts_of(acts, core), slice(None)
    )


def far_kernel(keep, where_ref, mate_ref, p1_ref, p2_ref, *refs):
    acts, outs = refs[:2], refs[2:]
    acc1, acc2 = outs[-2:]
    here, core = where_ref[0], where_ref[1]
    half = acc1.shape[1]
    cols = slice(0, half) if keep else slice(half, 2 * half)
    acc1[...] = p1_ref[:, cols]
    acc2[...] = p2_ref[:, cols]
    side = pieces_of(mate_ref)
    add_products(
        acc1, acc2, False, lambda j: side(lax.rem(here + j, NX)), acts_of(acts, 1 - core), cols
    )
    total = 2 * NY * NX * acts[0].shape[2]
    if keep:
        acc2[...] = acc2[...] / total
    else:
        outs[0][0] = acc1[...].astype(BF16)
        outs[0][1] = (acc2[...] / total).astype(BF16)


def near_products(where, mine, acts):
    pairs, _, piece, width = mine.shape
    shape = jax.ShapeDtypeStruct((pairs * piece, acts[0].shape[-1]), F32)
    return pl.pallas_call(
        near_kernel,
        out_shape=(shape, shape),
        in_specs=[SMEM] + [VMEM] * 3,
        out_specs=(VMEM, VMEM),
        compiler_params=params(),
        cost_estimate=cost(4 * 448 * 1024 * 512, 5 * 2**20),
        name="near_products",
    )(where, mine, *acts)


def far_products(keep, where, mate, p1, p2, acts):
    crows, cols = p1.shape
    shape = jax.ShapeDtypeStruct((crows, cols // 2), F32)
    return pl.pallas_call(
        functools.partial(far_kernel, keep),
        out_shape=(shape, shape) if keep else jax.ShapeDtypeStruct((2, crows, cols // 2), BF16),
        in_specs=[SMEM] + [VMEM] * 5,
        out_specs=(VMEM, VMEM) if keep else VMEM,
        scratch_shapes=[] if keep else [pltpu.VMEM((crows, cols // 2), F32)] * 2,
        compiler_params=params(),
        cost_estimate=cost(2 * 448 * 1024 * 512, 5 * 2**20),
        name="far_products",
    )(where, mate, p1, p2, *acts)


def added(*values):
    total = values[0].astype(F32)
    for v in values[1:]:
        total = total + v.astype(F32)
    return total.astype(BF16)


def own_columns(value, parity):
    rows = [((i + 1) % NY * 2 + 1, i * 2 + 1) for i in range(NY)]
    first = jnp.where(parity == 0, value, lax.ppermute(value, ("y", "p"), rows))
    rows = [((i + 2 + p) % NY * 2 + p, i * 2 + p) for i in range(NY) for p in range(2)]
    return [first, lax.ppermute(value, ("y", "p"), rows)]


def body(activations, act_basis, out_grads, grad_basis):
    x, y, core, parity = (lax.axis_index(a) for a in ("x", "y", "c", "p"))
    swap = lambda v, axis: lax.ppermute(v, axis, [(0, 1), (1, 0)])
    pack = lambda *v: jnp.stack(v).astype(jnp.int32)
    gather = lambda v, axis: lax.all_gather(v, axis, axis=0, tiled=False)
    acts = lax.dot_general(
        activations, act_basis, (((1,), (1,)), ((), ())), preferred_element_type=F32
    ).astype(BF16)
    depth = out_grads.shape[1]
    payload = jnp.concatenate([out_grads, acts], axis=1)
    crossed = swap(payload, "h")
    turn, grad_basis, out_grads = lax.optimization_barrier(
        (swap(acts[:16, :128], "c"), grad_basis, out_grads)
    )
    basis = [grad_basis] + [from_rel(grad_basis, "x", j, NX) for j in (1, 2, 3)]
    tokens = [gather(out_grads, "y"), gather(crossed[:, :depth], "y")]
    acts = jnp.stack([acts, crossed[:, depth:]])
    acts = jnp.concatenate([acts, swap(acts, "p")], axis=-1)
    *tokens, acts = lax.optimization_barrier((*tokens, acts))

    here, there = pack(x, y, core, parity), pack(x, y, 1 - core, parity)
    got = swap(block_sums(1, there, tokens, basis, turn), "c")
    other = added(block_sums(1, here, tokens, basis, turn), got)
    other, acts, *tokens = lax.optimization_barrier((other, acts, *tokens))
    pair = swap(other, "p")
    got = swap(block_sums(0, there, tokens, basis, turn), "c")
    acts = jnp.stack([acts] + [from_rel(acts, "x", j, NX) for j in (1, 2, 3)])
    partial = added(block_sums(0, here, tokens, basis, turn), got, pair)
    partial, acts = lax.optimization_barrier((partial, acts))
    all_acts = own_columns(acts, parity)
    crows, width = partial.shape[1:]
    spread = lax.all_to_all(
        partial.reshape(NX * NM, crows // NM, width), ("x", "m"), split_axis=0, concat_axis=0, tiled=True
    ).reshape(NX, NM, crows // NM, width)
    own = added(*[spread[:, j] for j in range(NM)])
    own, all_acts = lax.optimization_barrier((own, all_acts))
    mine = gather(own, "m")
    mate = swap(mine, "c")
    where = pack(x, core)
    p1, p2 = near_products(where, mine, all_acts)
    away = swap(far_products(False, where, mate, p1, p2, all_acts), "p")
    grad, scale = far_products(True, where, mate, p1, p2, all_acts)
    return grad + away[0].astype(F32), scale + away[1].astype(F32)


def solution(mesh):
    fine = Mesh(mesh.devices.reshape(NY, 2, NX, NM, 2, 2), ("y", "h", "x", "m", "p", "c"))
    dp, tensor = ("y", "h", "x"), ("m", "p", "c")
    return jax.shard_map(
        body,
        mesh=fine,
        in_specs=(P(dp, None), P(tensor, None), P(dp, tensor), P(dp, tensor)),
        out_specs=(P(dp, tensor), P(dp, tensor)),
        check_vma=False,
    )
```

```python
import functools

import jax
import jax.numpy as jnp
from jax import lax
from jax.experimental import pallas as pl
from jax.experimental.pallas import tpu as pltpu
from jax.sharding import Mesh, PartitionSpec as P

F32 = jnp.float32
BF16 = jnp.bfloat16
NX, NY, NM = 4, 4, 4
VMEM = pl.BlockSpec(memory_space=pltpu.VMEM)
ANY = pl.BlockSpec(memory_space=pl.ANY)
SMEM = pl.BlockSpec(memory_space=pltpu.SMEM)


def params():
    return pltpu.CompilerParams(vmem_limit_bytes=24 * 1024 * 1024)


def cost(flops, nbytes):
    return pl.CostEstimate(flops=flops, bytes_accessed=nbytes, transcendentals=0)


def from_rel(value, axis, step, size):
    return lax.ppermute(value, axis, [((i + step) % size, i) for i in range(size)])


def block_kernel(rel, where_ref, *refs):
    tokens, basis = refs[:2], refs[2 : 2 + NX]
    out_ref, held_ref = refs[3 + NX :]
    here, y, half, parity = (where_ref[i] for i in range(4))
    rows = tokens[0].shape[1]
    for side in range(2):

        @pl.when(half == side)
        def _():
            for n in range(2):
                source = lax.rem(y + lax.rem(parity + rel, 2) + 2 * n, NY)
                held_ref[pl.ds(n * rows, rows)] = tokens[side][source]

    for j in range(NX):
        home = lax.rem(here + j, NX)
        sums = lax.dot_general(
            basis[j][...], held_ref[...], (((1,), (1,)), ((), ())), preferred_element_type=F32
        ).astype(BF16)
        piece = sums.shape[0] // NM
        for m in range(NM):
            out_ref[m, home] = sums[m * piece : (m + 1) * piece]


def block_sums(rel, where, tokens, basis, turn):
    _, rows, depth = tokens[0].shape
    crows = basis[0].shape[0]
    return pl.pallas_call(
        functools.partial(block_kernel, rel),
        out_shape=jax.ShapeDtypeStruct((NM, NX, crows // NM, 2 * rows), BF16),
        in_specs=[SMEM] + [VMEM] * (2 + NX) + [ANY],
        out_specs=VMEM,
        scratch_shapes=[pltpu.VMEM((2 * rows, depth), BF16)],
        compiler_params=params(),
        cost_estimate=cost(2 * NX * crows * 2 * rows * depth, 6 * 2**20),
        name="block_sums",
    )(where, *tokens, *basis, turn)


def add_products(out1, out2, first, pieces, acts, cols):
    for j in range(NX):
        g, a = pieces(j), acts(j)[:, cols]
        gw, aw = g.astype(F32), a.astype(F32)
        g2, a2 = (gw * gw).astype(BF16), (aw * aw).astype(BF16)
        p1 = jnp.dot(g, a, preferred_element_type=F32)
        p2 = jnp.dot(g2, a2, preferred_element_type=F32)
        if first and j == 0:
            out1[...] = p1
            out2[...] = p2
        else:
            out1[...] += p1
            out2[...] += p2


def pieces_of(ref):
    pairs, _, piece, width = ref.shape
    return lambda j: ref[:, j].reshape(pairs * piece, width)


def acts_of(refs, half):
    return lambda j: jnp.concatenate([r[j, half] for r in refs], axis=0)


def near_kernel(where_ref, mine_ref, *refs):
    acts, (p1_ref, p2_ref) = refs[:2], refs[2:]
    here, core = where_ref[0], where_ref[1]
    side = pieces_of(mine_ref)
    add_products(
        p1_ref, p2_ref, True, lambda j: side(lax.rem(here + j, NX)), acts_of(acts, core), slice(None)
    )


def far_kernel(keep, where_ref, mate_ref, p1_ref, p2_ref, *refs):
    acts, outs = refs[:2], refs[2:]
    acc1, acc2 = outs[-2:]
    here, core = where_ref[0], where_ref[1]
    half = acc1.shape[1]
    cols = slice(0, half) if keep else slice(half, 2 * half)
    acc1[...] = p1_ref[:, cols]
    acc2[...] = p2_ref[:, cols]
    side = pieces_of(mate_ref)
    add_products(
        acc1, acc2, False, lambda j: side(lax.rem(here + j, NX)), acts_of(acts, 1 - core), cols
    )
    total = 2 * NY * NX * acts[0].shape[2]
    if keep:
        acc2[...] = acc2[...] / total
    else:
        outs[0][0] = acc1[...].astype(BF16)
        outs[0][1] = (acc2[...] / total).astype(BF16)


def near_products(where, mine, acts):
    pairs, _, piece, width = mine.shape
    shape = jax.ShapeDtypeStruct((pairs * piece, acts[0].shape[-1]), F32)
    return pl.pallas_call(
        near_kernel,
        out_shape=(shape, shape),
        in_specs=[SMEM] + [VMEM] * 3,
        out_specs=(VMEM, VMEM),
        compiler_params=params(),
        cost_estimate=cost(4 * 448 * 1024 * 512, 5 * 2**20),
        name="near_products",
    )(where, mine, *acts)


def far_products(keep, where, mate, p1, p2, acts):
    crows, cols = p1.shape
    shape = jax.ShapeDtypeStruct((crows, cols // 2), F32)
    return pl.pallas_call(
        functools.partial(far_kernel, keep),
        out_shape=(shape, shape) if keep else jax.ShapeDtypeStruct((2, crows, cols // 2), BF16),
        in_specs=[SMEM] + [VMEM] * 5,
        out_specs=(VMEM, VMEM) if keep else VMEM,
        scratch_shapes=[] if keep else [pltpu.VMEM((crows, cols // 2), F32)] * 2,
        compiler_params=params(),
        cost_estimate=cost(2 * 448 * 1024 * 512, 5 * 2**20),
        name="far_products",
    )(where, mate, p1, p2, *acts)


def added(*values):
    total = values[0].astype(F32)
    for v in values[1:]:
        total = total + v.astype(F32)
    return total.astype(BF16)


def own_columns(value, parity):
    rows = [((i + 1) % NY * 2 + 1, i * 2 + 1) for i in range(NY)]
    first = jnp.where(parity == 0, value, lax.ppermute(value, ("y", "p"), rows))
    rows = [((i + 2 + p) % NY * 2 + p, i * 2 + p) for i in range(NY) for p in range(2)]
    return [first, lax.ppermute(value, ("y", "p"), rows)]


def body(activations, act_basis, out_grads, grad_basis):
    x, y, core, parity = (lax.axis_index(a) for a in ("x", "y", "c", "p"))
    swap = lambda v, axis: lax.ppermute(v, axis, [(0, 1), (1, 0)])
    pack = lambda *v: jnp.stack(v).astype(jnp.int32)
    gather = lambda v, axis: lax.all_gather(v, axis, axis=0, tiled=False)
    acts = lax.dot_general(
        activations, act_basis, (((1,), (1,)), ((), ())), preferred_element_type=F32
    ).astype(BF16)
    depth = out_grads.shape[1]
    payload = jnp.concatenate([out_grads, acts], axis=1)
    crossed = swap(payload, "h")
    turn, grad_basis, out_grads = lax.optimization_barrier(
        (swap(acts[:16, :128], "c"), grad_basis, out_grads)
    )
    basis = [grad_basis] + [from_rel(grad_basis, "x", j, NX) for j in (1, 2, 3)]
    tokens = [gather(out_grads, "y"), gather(crossed[:, :depth], "y")]
    acts = jnp.stack([acts, crossed[:, depth:]])
    acts = jnp.concatenate([acts, swap(acts, "p")], axis=-1)
    *tokens, acts = lax.optimization_barrier((*tokens, acts))

    here, there = pack(x, y, core, parity), pack(x, y, 1 - core, parity)
    got = swap(block_sums(1, there, tokens, basis, turn), "c")
    other = added(block_sums(1, here, tokens, basis, turn), got)
    other, acts, *tokens = lax.optimization_barrier((other, acts, *tokens))
    pair = swap(other, "p")
    got = swap(block_sums(0, there, tokens, basis, turn), "c")
    acts = jnp.stack([acts] + [from_rel(acts, "x", j, NX) for j in (1, 2, 3)])
    partial = added(block_sums(0, here, tokens, basis, turn), got, pair)
    partial, acts = lax.optimization_barrier((partial, acts))
    all_acts = own_columns(acts, parity)
    piece, width = partial.shape[2:]
    spread = lax.all_to_all(
        partial.reshape(NM * NX, piece, width), ("m", "x"), split_axis=0, concat_axis=0, tiled=True
    ).reshape(NM, NX, piece, width)
    own = added(*[spread[j] for j in range(NM)])
    own, all_acts = lax.optimization_barrier((own, all_acts))
    mine = gather(own, "m")
    mate = swap(mine, "c")
    where = pack(x, core)
    p1, p2 = near_products(where, mine, all_acts)
    away = swap(far_products(False, where, mate, p1, p2, all_acts), "p")
    grad, scale = far_products(True, where, mate, p1, p2, all_acts)
    return grad + away[0].astype(F32), scale + away[1].astype(F32)


def solution(mesh):
    fine = Mesh(mesh.devices.reshape(NY, 2, NX, NM, 2, 2), ("y", "h", "x", "m", "p", "c"))
    dp, tensor = ("y", "h", "x"), ("m", "p", "c")
    return jax.shard_map(
        body,
        mesh=fine,
        in_specs=(P(dp, None), P(tensor, None), P(dp, tensor), P(dp, tensor)),
        out_specs=(P(dp, tensor), P(dp, tensor)),
        check_vma=False,
    )
```

```python
import functools

import jax
import jax.numpy as jnp
from jax import lax
from jax.experimental import pallas as pl
from jax.experimental.pallas import tpu as pltpu
from jax.sharding import Mesh, PartitionSpec as P

F32 = jnp.float32
BF16 = jnp.bfloat16
NX, NY, NM = 4, 4, 4
VMEM = pl.BlockSpec(memory_space=pltpu.VMEM)
ANY = pl.BlockSpec(memory_space=pl.ANY)
SMEM = pl.BlockSpec(memory_space=pltpu.SMEM)


def params():
    return pltpu.CompilerParams(vmem_limit_bytes=24 * 1024 * 1024)


def cost(flops, nbytes):
    return pl.CostEstimate(flops=flops, bytes_accessed=nbytes, transcendentals=0)


def from_rel(value, axis, step, size):
    return lax.ppermute(value, axis, [((i + step) % size, i) for i in range(size)])


def block_kernel(rel, where_ref, *refs):
    tokens, basis = refs[:2], refs[2 : 2 + NX]
    out_ref, held_ref = refs[3 + NX :]
    here, y, half, parity = (where_ref[i] for i in range(4))
    rows = tokens[0].shape[1]
    for side in range(2):

        @pl.when(half == side)
        def _():
            for n in range(2):
                source = lax.rem(y + lax.rem(parity + rel, 2) + 2 * n, NY)
                held_ref[pl.ds(n * rows, rows)] = tokens[side][source]

    for j in range(NX):
        home = lax.rem(here + j, NX)
        sums = lax.dot_general(
            basis[j][...], held_ref[...], (((1,), (1,)), ((), ())), preferred_element_type=F32
        ).astype(BF16)
        piece = sums.shape[0] // NM
        for m in range(NM):
            out_ref[m, home] = sums[m * piece : (m + 1) * piece]


def block_sums(rel, where, tokens, basis, turn):
    _, rows, depth = tokens[0].shape
    crows = basis[0].shape[0]
    return pl.pallas_call(
        functools.partial(block_kernel, rel),
        out_shape=jax.ShapeDtypeStruct((NM, NX, crows // NM, 2 * rows), BF16),
        in_specs=[SMEM] + [VMEM] * (2 + NX) + [ANY],
        out_specs=VMEM,
        scratch_shapes=[pltpu.VMEM((2 * rows, depth), BF16)],
        compiler_params=params(),
        cost_estimate=cost(2 * NX * crows * 2 * rows * depth, 6 * 2**20),
        name="block_sums",
    )(where, *tokens, *basis, turn)


def add_products(out1, out2, first, pieces, acts, cols):
    for j in range(NX):
        g, a = pieces(j), acts(j)[:, cols]
        gw, aw = g.astype(F32), a.astype(F32)
        g2, a2 = (gw * gw).astype(BF16), (aw * aw).astype(BF16)
        p1 = jnp.dot(g, a, preferred_element_type=F32)
        p2 = jnp.dot(g2, a2, preferred_element_type=F32)
        if first and j == 0:
            out1[...] = p1
            out2[...] = p2
        else:
            out1[...] += p1
            out2[...] += p2


def pieces_of(ref):
    pairs, _, piece, width = ref.shape
    return lambda j: ref[:, j].reshape(pairs * piece, width)


def acts_of(refs, half):
    return lambda j: jnp.concatenate([r[j, half] for r in refs], axis=0)


def near_kernel(where_ref, mine_ref, *refs):
    acts, (p1_ref, p2_ref) = refs[:2], refs[2:]
    here, core = where_ref[0], where_ref[1]
    side = pieces_of(mine_ref)
    add_products(
        p1_ref, p2_ref, True, lambda j: side(lax.rem(here + j, NX)), acts_of(acts, core), slice(None)
    )


def far_kernel(where_ref, mate_ref, p1_ref, p2_ref, *refs):
    acts, (acc1, acc2) = refs[:2], refs[2:]
    here, core = where_ref[0], where_ref[1]
    half = acc1.shape[1]
    cols = slice(0, half)
    acc1[...] = p1_ref[:, cols]
    acc2[...] = p2_ref[:, cols]
    side = pieces_of(mate_ref)
    add_products(
        acc1, acc2, False, lambda j: side(lax.rem(here + j, NX)), acts_of(acts, 1 - core), cols
    )
    total = 2 * NY * NX * acts[0].shape[2]
    acc2[...] = acc2[...] / total


def near_products(where, mine, acts):
    pairs, _, piece, width = mine.shape
    shape = jax.ShapeDtypeStruct((pairs * piece, acts[0].shape[-1]), F32)
    return pl.pallas_call(
        near_kernel,
        out_shape=(shape, shape),
        in_specs=[SMEM] + [VMEM] * 3,
        out_specs=(VMEM, VMEM),
        compiler_params=params(),
        cost_estimate=cost(4 * 448 * 1024 * 512, 5 * 2**20),
        name="near_products",
    )(where, mine, *acts)


def far_products(where, mate, p1, p2, acts):
    crows, cols = p1.shape
    shape = jax.ShapeDtypeStruct((crows, cols // 2), F32)
    return pl.pallas_call(
        far_kernel,
        out_shape=(shape, shape),
        in_specs=[SMEM] + [VMEM] * 5,
        out_specs=(VMEM, VMEM),
        compiler_params=params(),
        cost_estimate=cost(2 * 448 * 1024 * 512, 5 * 2**20),
        name="far_products",
    )(where, mate, p1, p2, *acts)


def away_kernel(squares, where_ref, mate_ref, partial_ref, acts0_ref, acts1_ref, out_ref, acc_ref):
    here, core = where_ref[0], where_ref[1]
    half = acc_ref.shape[1]
    acc_ref[...] = partial_ref[:, half:]
    acts = acts_of((acts0_ref, acts1_ref), 1 - core)
    side = pieces_of(mate_ref)
    for j in range(NX):
        g, a = side(lax.rem(here + j, NX)), acts(j)[:, half:]
        if squares:
            gw, aw = g.astype(F32), a.astype(F32)
            g, a = (gw * gw).astype(BF16), (aw * aw).astype(BF16)
        acc_ref[...] += jnp.dot(g, a, preferred_element_type=F32)
    total = 2 * NY * NX * acts0_ref.shape[2] if squares else 1
    out_ref[...] = (acc_ref[...] / total).astype(BF16)


def away_products(squares, where, mate, partial, acts):
    crows, cols = partial.shape
    return pl.pallas_call(
        functools.partial(away_kernel, squares),
        out_shape=jax.ShapeDtypeStruct((crows, cols // 2), BF16),
        in_specs=[SMEM] + [VMEM] * 4,
        out_specs=VMEM,
        scratch_shapes=[pltpu.VMEM((crows, cols // 2), F32)],
        compiler_params=params(),
        cost_estimate=cost(448 * 1024 * 512, 4 * 2**20),
        name="away_products",
    )(where, mate, partial, *acts)


def added(*values):
    total = values[0].astype(F32)
    for v in values[1:]:
        total = total + v.astype(F32)
    return total.astype(BF16)


def own_columns(value, parity):
    rows = [((i + 1) % NY * 2 + 1, i * 2 + 1) for i in range(NY)]
    first = jnp.where(parity == 0, value, lax.ppermute(value, ("y", "p"), rows))
    rows = [((i + 2 + p) % NY * 2 + p, i * 2 + p) for i in range(NY) for p in range(2)]
    return [first, lax.ppermute(value, ("y", "p"), rows)]


def body(activations, act_basis, out_grads, grad_basis):
    x, y, core, parity = (lax.axis_index(a) for a in ("x", "y", "c", "p"))
    swap = lambda v, axis: lax.ppermute(v, axis, [(0, 1), (1, 0)])
    pack = lambda *v: jnp.stack(v).astype(jnp.int32)
    gather = lambda v, axis: lax.all_gather(v, axis, axis=0, tiled=False)
    acts = lax.dot_general(
        activations, act_basis, (((1,), (1,)), ((), ())), preferred_element_type=F32
    ).astype(BF16)
    depth = out_grads.shape[1]
    payload = jnp.concatenate([out_grads, acts], axis=1)
    crossed = swap(payload, "h")
    turn, grad_basis, out_grads = lax.optimization_barrier(
        (swap(acts[:16, :128], "c"), grad_basis, out_grads)
    )
    basis = [grad_basis] + [from_rel(grad_basis, "x", j, NX) for j in (1, 2, 3)]
    tokens = [gather(out_grads, "y"), gather(crossed[:, :depth], "y")]
    acts = jnp.stack([acts, crossed[:, depth:]])
    acts = jnp.concatenate([acts, swap(acts, "p")], axis=-1)
    *tokens, acts = lax.optimization_barrier((*tokens, acts))

    here, there = pack(x, y, core, parity), pack(x, y, 1 - core, parity)
    got = swap(block_sums(1, there, tokens, basis, turn), "c")
    other = added(block_sums(1, here, tokens, basis, turn), got)
    other, acts, *tokens = lax.optimization_barrier((other, acts, *tokens))
    pair = swap(other, "p")
    got = swap(block_sums(0, there, tokens, basis, turn), "c")
    acts = jnp.stack([acts] + [from_rel(acts, "x", j, NX) for j in (1, 2, 3)])
    partial = added(block_sums(0, here, tokens, basis, turn), got, pair)
    partial, acts = lax.optimization_barrier((partial, acts))
    all_acts = own_columns(acts, parity)
    piece, width = partial.shape[2:]
    spread = lax.all_to_all(
        partial.reshape(NM * NX, piece, width), ("m", "x"), split_axis=0, concat_axis=0, tiled=True
    ).reshape(NM, NX, piece, width)
    own = added(*[spread[j] for j in range(NM)])
    own, all_acts = lax.optimization_barrier((own, all_acts))
    mine = gather(own, "m")
    mate = swap(mine, "c")
    where = pack(x, core)
    p1, p2 = near_products(where, mine, all_acts)
    grad_away = swap(away_products(False, where, mate, p1, all_acts), "p")
    scale_away = swap(away_products(True, where, mate, p2, all_acts), "p")
    grad, scale = far_products(where, mate, p1, p2, all_acts)
    return grad + grad_away.astype(F32), scale + scale_away.astype(F32)


def solution(mesh):
    fine = Mesh(mesh.devices.reshape(NY, 2, NX, NM, 2, 2), ("y", "h", "x", "m", "p", "c"))
    dp, tensor = ("y", "h", "x"), ("m", "p", "c")
    return jax.shard_map(
        body,
        mesh=fine,
        in_specs=(P(dp, None), P(tensor, None), P(dp, tensor), P(dp, tensor)),
        out_specs=(P(dp, tensor), P(dp, tensor)),
        check_vma=False,
    )
```
